512 devices in a mesh: dp: 512 (over z, x, y, core).
Axes of the slice: x: 4, y: 8, z: 8, core: 2. Of those that a mesh axis runs over, the one named last changes fastest.
Arguments:
- image: bfloat16 [65536, 1152], P('dp')
- text: bfloat16 [65536, 1152], P('dp')
- plan: int32 [5, 512], replicated, may hold values from 0 to 511, as said below
- offset: int32 [1], replicated, may hold values from 0 to 2
- logit_scale: float32 [1], replicated, may hold values from 16 to 64
- logit_bias: float32 [1], replicated, may hold values from -3 to 0
Outputs:
- row_loss: float32 [65536], P('dp')
- image_grad: float32 [65536, 1152], P('dp')
- text_grad: float32 [65536, 1152], P('dp')
The draws below stay inside these ranges and needn't reach their ends.
Inputs may be any that keep to these rules, and one draw needn't show every extreme that they name: `plan`: in every row r there is a bit b_r, different in each row, such that device p's partner is p XOR 2 ** b_r; in row 2 that bit is the highest one, so the partner is half the devices away.
All inputs are finite; a program needn't handle non-finite values.
Results may differ from the reference program's by a relative error of at most 0.0057.
Values may be sent and summed in bfloat16 or wider, within the bound.
A program may use at most 64 MiB of HBM per device.

```python
import math
import jax
import jax.numpy as jnp
from jax import lax

D = 1152
ROWS = 128
ROUNDS = 3
SCHED = 5
TOKENS = 65536
N_DP = 512


def embed_rows(key, spread):
    base_key, scale_key = jax.random.split(key, 2)
    values = jax.random.normal(base_key, (TOKENS, D), jnp.float32)
    levels = jax.random.uniform(scale_key, (TOKENS, 1), jnp.float32, 0.0, 1.0)
    return values * jnp.exp(levels * jnp.log(spread))


def draw_image(key, part):
    key = jax.random.fold_in(key, 11)
    values = embed_rows(key, 10.0)
    return values.astype(jnp.bfloat16)


def draw_text(key, part):
    key = jax.random.fold_in(key, 23)
    values = embed_rows(key, 10.0)
    return values.astype(jnp.bfloat16)


def draw_plan(key, part):
    key = jax.random.fold_in(key, 37)
    bit_count = N_DP.bit_length() - 1
    lower = jax.random.permutation(key, bit_count - 1).astype(jnp.int32)
    top_bit = jnp.full((1,), bit_count - 1, jnp.int32)
    chosen = jnp.concatenate([lower[:2], top_bit, lower[2:4]])[:SCHED].astype(jnp.int32)
    masks = jnp.left_shift(jnp.ones_like(chosen), chosen)
    devices = jnp.arange(N_DP, dtype=jnp.int32)
    return jnp.bitwise_xor(devices[None, :], masks[:, None]).astype(jnp.int32)


def setup_inputs(seed: int = 0) -> dict:
    seeds = jax.random.split(jax.random.key(seed), 7)
    return {
        "image": draw_image(jax.random.fold_in(seeds[6], 71), 0),
        "text": draw_text(jax.random.fold_in(seeds[6], 71), 0),
        "plan": draw_plan(jax.random.fold_in(seeds[6], 71), 0),
        "offset": jax.random.randint(seeds[3], (1,), 0, SCHED - ROUNDS + 1).astype(jnp.int32),
        "logit_scale": jnp.clip(jnp.exp(jax.random.uniform(seeds[4], (1,), jnp.float32, math.log(16.0), math.log(64.0))), 16.0, 64.0),
        "logit_bias": jnp.clip(jax.random.uniform(seeds[5], (1,), jnp.float32, -3.0, 0.0), -3.0, 0.0),
    }


def unit_rows(values):
    whole = values.astype(jnp.float32)
    norms = jnp.sqrt(lax.optimization_barrier(jnp.sum(whole * whole, axis=-1, keepdims=True)) + 1e-06)
    return (whole / norms, norms)

def block_terms(img_block, txt_block, labels, scale_val, bias_val):
    logits = scale_val * jnp.einsum('nid,njd->nij', img_block, txt_block, precision=lax.Precision.HIGHEST) + bias_val
    coef_low = (-labels * jax.nn.sigmoid(-labels * logits)).astype(jnp.bfloat16)
    coef = lax.optimization_barrier(coef_low).astype(jnp.float32)
    losses = lax.optimization_barrier(jnp.sum(jax.nn.softplus(-labels * logits), axis=-1))
    img_part = scale_val * jnp.einsum('nij,njd->nid', coef, txt_block, precision=lax.Precision.HIGHEST)
    txt_part = scale_val * jnp.einsum('nij,nid->njd', coef, img_block, precision=lax.Precision.HIGHEST)
    return (losses, img_part, txt_part)

def finish(direction, unit_exact, norms):
    inner = lax.optimization_barrier(jnp.sum(unit_exact * direction, axis=-1, keepdims=True))
    return (direction - unit_exact * inner) / norms

def reference(image, text, plan, offset, logit_scale, logit_bias):
    img_exact, img_norm = unit_rows(image)
    txt_exact, txt_norm = unit_rows(text)
    img_unit = img_exact.astype(jnp.bfloat16).astype(jnp.float32).reshape(N_DP, ROWS, D)
    txt_unit = txt_exact.astype(jnp.bfloat16).astype(jnp.float32).reshape(N_DP, ROWS, D)
    scale_val = logit_scale[0]
    bias_val = logit_bias[0]
    diagonal = jnp.eye(ROWS, dtype=jnp.float32)
    labels = 2.0 * diagonal - 1.0
    losses, img_dir, txt_dir = block_terms(img_unit, txt_unit, labels[None], scale_val, bias_val)
    for round_idx in range(ROUNDS):
        partner = lax.dynamic_index_in_dim(plan, offset[0] + round_idx, 0, keepdims=False).astype(jnp.int32)
        txt_other = txt_unit[partner]
        more_loss, img_part, txt_part = block_terms(img_unit, txt_other, jnp.float32(-1.0), scale_val, bias_val)
        losses = losses + more_loss
        img_dir = img_dir + img_part
        txt_low = txt_part.astype(jnp.bfloat16)
        txt_back = lax.optimization_barrier(txt_low).astype(jnp.float32)
        txt_dir = txt_dir.at[partner].add(txt_back)
    image_grad = finish(img_dir.reshape(TOKENS, D), img_exact, img_norm)
    text_grad = finish(txt_dir.reshape(TOKENS, D), txt_exact, txt_norm)
    return (losses.reshape(TOKENS), image_grad, text_grad)
```

```python
import functools

import jax
import jax.numpy as jnp
from jax import lax
from jax.experimental import pallas as pl
from jax.experimental.pallas import tpu as pltpu
from jax.sharding import PartitionSpec as P

MESH = pl.DeviceIdType.MESH
ROUNDS = 3
ROWS = 128
BOTH = 2 * ROWS
CHUNKS = 8
SLICE = BOTH // CHUNKS
PIECE = 2 * SLICE
PIECES = BOTH // PIECE
STEPS = 3 * CHUNKS
TOP_BIT = 8
RINGS = ((6, 3), (1, 3), (4, 2))
WINDOWS = tuple((low, high) for high in range(TOP_BIT) for low in range(high))


def div(a, b):
    return lax.div(a, jnp.int32(b))


def rem(a, b):
    return lax.rem(a, jnp.int32(b))


def pick(index, table):
    value = jnp.int32(table[0])
    for k in range(1, len(table)):
        if table[k] != table[k - 1]:
            value = jnp.where(index >= k, jnp.int32(table[k]), value)
    return value


class Direct:
    buffers = 1
    phases = 0
    final = 0

    def __init__(self, bit):
        self.bit = bit

    def place(self, me):
        mask = 1 << self.bit
        self.partner = me + (1 - 2 * rem(div(me, mask), 2)) * mask

    def neighbours(self):
        return [self.partner]

    def first(self, chunk):
        return 0, self.partner


class Relay:
    def __init__(self, ring, kind, hops):
        self.bit, count = ring
        self.size = 1 << count
        self.kind = kind
        self.phases = hops - 1
        self.buffers = 6 if kind == "two" else hops
        self.final = self.buffers - 1

    def place(self, me):
        self.me = me
        self.at = rem(div(me, 1 << self.bit), self.size)
        self.low = rem(div(self.at, 2), 2)
        self.mid = rem(div(self.at + 1, 2), 2)

    def device(self, step):
        return self.me + (rem(self.at + step + self.size, self.size) - self.at) * (1 << self.bit)

    def neighbours(self):
        return [self.device(1), self.device(-1)]

    def first(self, chunk):
        if self.kind == "both":
            return 0, self.device(1 - 2 * rem(chunk, 2))
        if self.kind == "one":
            return 0, self.device(1 - 2 * rem(self.at, 2))
        return self.low, self.device(1 - 2 * self.low)

    def hop(self, phase, chunk):
        if self.kind == "both":
            return phase - 1, phase, self.device(1 - 2 * rem(chunk, 2))
        if self.kind == "one":
            return phase - 1, phase, self.device(1 - 2 * rem(self.at + phase, 2))
        low, mid = self.low, self.mid
        ahead = 1 - 2 * low
        second = phase == 2
        here = jnp.where(
            mid == 1,
            jnp.where(phase == 1, 1 - low, jnp.where(second, low, 2)),
            jnp.where(phase == 1, 2, jnp.where(second, 3 + low, 4 - low)),
        )
        there = jnp.where(mid == 1, jnp.where(phase == 3, 4 - low, 2), jnp.where(phase == 1, 4 - low, 5))
        return here, there, self.device(jnp.where(second, ahead, -ahead))


def routes(bits):
    flows, blocks = [], []

    def direct(bit, how):
        flows.append(Direct(bit))
        blocks.append((flows[-1], 0, how))

    for ring in RINGS:
        first, count = ring
        held = tuple(b - first for b in bits if first <= b < first + count)
        if count == 3 and 2 in held:
            kind = "two" if 1 in held else "one" if 0 in held else "both"
            flow = Relay(ring, kind, 4)
            flows.append(flow)
            blocks.append((flow, flow.final, "last" if first + 2 == TOP_BIT else "late"))
            if kind == "two":
                blocks.append((flow, 2, "passed two"))
                if 0 in held:
                    direct(first, "after")
            elif kind == "one":
                blocks.append((flow, 0, "passed one"))
        elif count == 2 and len(held) == 2:
            flow = Relay(ring, "one", 2)
            flows.append(flow)
            blocks.append((flow, flow.final, "early"))
            blocks.append((flow, 0, "passed one"))
        else:
            for low in held:
                direct(first + low, "late" if count == 3 and 1 in held else "early")
    if 0 in bits:
        direct(0, "early")
    return flows, blocks


def agenda(kind, blocks):
    tasks = [(piece, 0, piece) for piece in range(PIECES)]
    early = 0
    for number, (_, _, how) in enumerate(blocks, 1):
        if how == "last":
            steps = {"both": (24, 24, 24, 24), "one": (20, 21, 22, 23), "two": (19, 21, 23, 24)}[kind]
        elif how == "passed two":
            steps = (17, 19, 21, 23)
        elif how == "passed one":
            steps = (4, 5, 6, 7) if kind == "one" else (9, 10, 11, 12)
        elif how == "early":
            steps = (16, 18, 20, 22) if kind == "two" else tuple(16 + 4 * early + k for k in range(4))
            early += 1
        elif how == "late":
            steps = (24, 24, 24, 24) if kind == "both" else (21, 22, 23, 24)
        else:
            steps = (24, 24, 24, 24)
        tasks += [(step, number, piece) for piece, step in enumerate(steps)]
    after = [how == "after" for _, _, how in blocks]
    tasks.sort(key=lambda t: (t[0], t[1] > 0 and after[t[1] - 1], t[2], -t[1]))
    return tasks


def kernel(bits, img_hbm, txt_hbm, scale_ref, bias_ref, loss_out, img_out, txt_out,
           raw, norms, held, total, losses, load_sem, store_sem, send_sem, recv_sem):
    me = lax.axis_index("dp")
    flows, blocks = routes(bits)
    base = 1
    for number, flow in enumerate(flows):
        flow.place(me)
        flow.base, flow.sends = base, 4 * number
        base += flow.buffers

    loads = [
        pltpu.make_async_copy(src, raw.at[pl.ds(ROWS * k, ROWS)], load_sem.at[k])
        for k, src in enumerate((txt_hbm, img_hbm))
    ]
    for load in loads:
        load.start()
    barrier = pltpu.get_barrier_semaphore()
    greeted = [d for flow in flows for d in flow.neighbours()]
    for device in greeted:
        pl.semaphore_signal(barrier, inc=1, device_id=(device,), device_id_type=MESH)
    for load in loads:
        load.wait()

    def rows(start, count):
        return pl.ds(pl.multiple_of(start, count), count)

    @pl.loop(0, CHUNKS)
    def _(chunk):
        part = rows(chunk * SLICE, SLICE)
        whole = raw[part, :].astype(jnp.float32)
        norm = jnp.sqrt(jnp.sum(whole * whole, axis=-1, keepdims=True) + 1e-06)
        norms[part, :] = norm
        held[0, part, :] = (whole / norm).astype(jnp.bfloat16)
        total[part, :] = jnp.zeros_like(whole)

    losses[...] = jnp.zeros_like(losses)
    pl.semaphore_wait(barrier, len(greeted))

    def copy(here, there, chunk, send, device):
        part = rows(chunk * SLICE, SLICE)
        return pltpu.make_async_remote_copy(
            src_ref=held.at[here, part],
            dst_ref=held.at[there, part],
            send_sem=send_sem.at[send],
            recv_sem=recv_sem.at[there, chunk],
            device_id=(device,),
            device_id_type=MESH,
        )

    def arrived(buffer, chunk):
        copy(0, buffer, chunk, 0, me).wait_recv()

    @pl.loop(0, CHUNKS)
    def _(chunk):
        for flow in flows:
            there, device = flow.first(chunk)
            copy(0, flow.base + there, chunk, flow.sends, device).start()

    scale, bias = scale_ref[0], bias_ref[0]
    far = next(flow for flow, _, how in blocks if how == "last")
    tasks = agenda(far.kind, blocks)
    where = [0] + [flow.base + buffer for flow, buffer, _ in blocks]
    open_ = [0] + [int(not how.startswith("passed")) for _, _, how in blocks]

    def pair(task):
        block = pick(task, [t[1] for t in tasks])
        piece = pick(task, [t[2] for t in tasks])
        buffer = pick(block, where)

        @pl.when(pick(block, open_) == 1)
        def _():
            arrived(buffer, 2 * piece)
            arrived(buffer, 2 * piece + 1)

        side = div(piece, PIECES // 2)
        mine = rows(ROWS - ROWS * side, ROWS)
        other = held[buffer, rows(piece * PIECE, PIECE), :]
        logits = scale * lax.dot_general(
            held[0, mine, :], other, (((1,), (1,)), ((), ())), preferred_element_type=jnp.float32
        ) + bias
        row = lax.broadcasted_iota(jnp.int32, logits.shape, 0)
        column = lax.broadcasted_iota(jnp.int32, logits.shape, 1) + rem(piece, PIECES // 2) * PIECE
        diagonal = row == jnp.where(block == 0, column, -1)
        logits = jnp.where(diagonal, -logits, logits)
        small = jnp.exp(-jnp.abs(logits))
        share = 1.0 / (1.0 + small)
        coef = jnp.where(logits >= 0, share, small * share)
        coef = jnp.where(diagonal, -coef, coef)
        loss = jnp.maximum(logits, 0.0) + jnp.log1p(small)
        losses[:, :PIECE] += jnp.where(side == 0, loss, 0.0)
        total[mine, :] += jnp.dot(coef.astype(jnp.bfloat16), other, preferred_element_type=jnp.float32)

    due = [sum(t[0] < step for t in tasks) for step in range(STEPS + 2)]

    @pl.loop(0, STEPS + 1)
    def _(step):
        phase = div(step, CHUNKS) + 1
        chunk = rem(step, CHUNKS)
        for flow in flows:
            if flow.phases:
                @pl.when(phase <= flow.phases)
                def _(flow=flow):
                    here, there, device = flow.hop(phase, chunk)
                    arrived(flow.base + here, chunk)
                    copy(flow.base + here, flow.base + there, chunk, flow.sends + phase, device).start()

        @pl.loop(pick(step, due), pick(step + 1, due))
        def _(task):
            pair(task)

    @pl.loop(0, CHUNKS)
    def _(chunk):
        part = rows(chunk * SLICE, SLICE)
        direction = scale * total[part, :]
        scaled = 1.0 / norms[part, :]
        unit = raw[part, :].astype(jnp.float32) * scaled
        inner = jnp.sum(unit * direction, axis=-1, keepdims=True)
        total[part, :] = (direction - unit * inner) * scaled

    stores = [
        pltpu.make_async_copy(total.at[pl.ds(ROWS * k, ROWS)], out, store_sem.at[k])
        for k, out in enumerate((txt_out, img_out))
    ]
    for store in stores:
        store.start()
    loss_out[...] = jnp.sum(losses[...].T, axis=0, keepdims=True)
    for flow in flows:
        for phase in range(flow.phases + 1):
            pltpu.make_async_remote_copy(
                src_ref=held.at[0], dst_ref=held.at[flow.base], send_sem=send_sem.at[flow.sends + phase],
                recv_sem=recv_sem.at[flow.base, 0], device_id=(me,), device_id_type=MESH,
            ).wait_send()
    for store in stores:
        store.wait()


def window(number, image, text, scale, bias):
    bits = (*WINDOWS[number], TOP_BIT)
    flows, _ = routes(bits)
    buffers = 1 + sum(flow.buffers for flow in flows)
    width = image.shape[1]
    any_space = pl.BlockSpec(memory_space=pl.ANY)
    scalar = pl.BlockSpec(memory_space=pltpu.SMEM)
    return pl.pallas_call(
        functools.partial(kernel, bits),
        out_shape=(
            jax.ShapeDtypeStruct((1, ROWS), jnp.float32),
            jax.ShapeDtypeStruct((ROWS, width), jnp.float32),
            jax.ShapeDtypeStruct((ROWS, width), jnp.float32),
        ),
        in_specs=[any_space, any_space, scalar, scalar],
        out_specs=(pl.BlockSpec(memory_space=pltpu.VMEM), any_space, any_space),
        scratch_shapes=[
            pltpu.VMEM((BOTH, width), jnp.bfloat16),
            pltpu.VMEM((BOTH, 1), jnp.float32),
            pltpu.VMEM((buffers, BOTH, width), jnp.bfloat16),
            pltpu.VMEM((BOTH, width), jnp.float32),
            pltpu.VMEM((ROWS, ROWS), jnp.float32),
            pltpu.SemaphoreType.DMA((2,)),
            pltpu.SemaphoreType.DMA((2,)),
            pltpu.SemaphoreType.DMA((4 * len(flows),)),
            pltpu.SemaphoreType.DMA((buffers, CHUNKS)),
        ],
        compiler_params=pltpu.CompilerParams(
            collective_id=number, has_side_effects=True, vmem_limit_bytes=24 << 20
        ),
        name="window",
    )(image, text, scale, bias)


def per_device(image, text, plan, offset, logit_scale, logit_bias):
    listed = jnp.arange(plan.shape[0], dtype=jnp.int32) - offset[0]
    others = jnp.sum(jnp.where((listed >= 0) & (listed < ROUNDS), plan[:, 0], 0)) - (1 << TOP_BIT)
    high = 31 - lax.clz(others)
    low = 31 - lax.clz(others - jnp.left_shift(jnp.int32(1), high))
    number = high * (high - 1) // 2 + low
    branches = [functools.partial(window, k) for k in range(len(WINDOWS))]
    losses, image_grad, text_grad = lax.switch(number, branches, image, text, logit_scale, logit_bias)
    return losses.reshape(ROWS), image_grad, text_grad


def solution(mesh):
    in_specs = (P("dp", None), P("dp", None), P(), P(), P(), P())
    out_specs = (P("dp"), P("dp", None), P("dp", None))
    return jax.shard_map(
        per_device, mesh=mesh, in_specs=in_specs, out_specs=out_specs, check_vma=False
    )
```

```python
import functools

import jax
import jax.numpy as jnp
from jax import lax
from jax.experimental import pallas as pl
from jax.experimental.pallas import tpu as pltpu
from jax.sharding import PartitionSpec as P

MESH = pl.DeviceIdType.MESH
ROUNDS = 3
ROWS = 128
BOTH = 2 * ROWS
CHUNKS = 8
SLICE = BOTH // CHUNKS
PIECE = ROWS
PIECES = BOTH // PIECE
HALF = CHUNKS // 2
STEPS = 3 * CHUNKS
TOP_BIT = 8
RINGS = ((6, 3), (1, 3), (4, 2))
WINDOWS = tuple((low, high) for high in range(TOP_BIT) for low in range(high))


def div(a, b):
    return lax.div(a, jnp.int32(b))


def rem(a, b):
    return lax.rem(a, jnp.int32(b))


def pick(index, table):
    value = jnp.int32(table[0])
    for k in range(1, len(table)):
        if table[k] != table[k - 1]:
            value = jnp.where(index >= k, jnp.int32(table[k]), value)
    return value


class Direct:
    buffers = 1
    phases = 0
    final = 0

    def __init__(self, bit):
        self.bit = bit

    def place(self, me):
        mask = 1 << self.bit
        self.partner = me + (1 - 2 * rem(div(me, mask), 2)) * mask

    def neighbours(self):
        return [self.partner]

    def first(self, chunk):
        return 0, self.partner


class Relay:
    size = 8
    phases = 3
    final = 3

    def __init__(self, bit, taps):
        self.bit = bit
        self.taps = taps
        self.buffers = 4 + len(taps)

    def place(self, me):
        self.me = me
        self.at = rem(div(me, 1 << self.bit), self.size)

    def device(self, step):
        return self.me + (rem(self.at + step + self.size, self.size) - self.at) * (1 << self.bit)

    def side(self, tap):
        return rem(div(self.at, 1 << tap), 2)

    def partner(self, tap):
        return self.me + (1 - 2 * self.side(tap)) * (1 << (self.bit + tap))

    def neighbours(self):
        return [self.device(1), self.device(-1)] + [self.partner(tap) for tap in self.taps if tap]

    def slot(self, hop, down, at):
        buffer = hop - 1
        for number, tap in enumerate(self.taps):
            other = (hop == 1 << tap) & (down == rem(div(at, 1 << tap), 2))
            buffer = jnp.where(other, 4 + number, buffer)
        return buffer

    def hop(self, phase, chunk):
        down = rem(chunk, 2)
        step = 1 - 2 * down
        there = rem(self.at + step + self.size, self.size)
        return self.slot(phase, down, self.at), self.slot(phase + 1, down, there), self.device(step)

    def first(self, chunk):
        _, there, device = self.hop(0, chunk)
        return there, device


def routes(bits):
    flows, blocks = [], []

    def direct(bit, how):
        flows.append(Direct(bit))
        blocks.append((flows[-1], 0, how))

    for first, count in RINGS:
        held = tuple(b - first for b in bits if first <= b < first + count)
        if count == 3 and 2 in held:
            flow = Relay(first, held[:-1])
            flows.append(flow)
            blocks.append((flow, flow.final, "last" if first + 2 == TOP_BIT else "late"))
            for tap in flow.taps:
                blocks.append((flow, (1 << tap) - 1, ("near", "far")[tap]))
        else:
            for low in held:
                direct(first + low, "late" if 1 in held and (count == 3 or len(held) == 2) else "early")
    if 0 in bits:
        direct(0, "early")
    return flows, blocks


def agenda(blocks):
    tasks = [(1 + 2 * piece, 0, piece) for piece in range(PIECES)]
    early = 0
    for number, (flow, _, how) in enumerate(blocks, 1):
        if how in ("early", "near"):
            steps = (16 + 4 * early, 18 + 4 * early)
            early += 1
        else:
            steps = (24 if flow.phases else 22, 24)
        tasks += [(step, number, piece) for piece, step in enumerate(steps)]
    tasks.sort(key=lambda t: (t[0], t[2], -t[1]))
    return tasks


def kernel(bits, img_hbm, txt_hbm, scale_ref, bias_ref, loss_out, img_out, txt_out,
           raw, norms, held, total, losses, load_sem, store_sem, send_sem, recv_sem):
    me = lax.axis_index("dp")
    flows, blocks = routes(bits)
    base = 1
    for number, flow in enumerate(flows):
        flow.place(me)
        flow.base, flow.sends = base, 6 * number
        base += flow.buffers

    loads = [
        pltpu.make_async_copy(src, raw.at[pl.ds(ROWS * k, ROWS)], load_sem.at[k])
        for k, src in enumerate((txt_hbm, img_hbm))
    ]
    for load in loads:
        load.start()
    barrier = pltpu.get_barrier_semaphore()
    greeted = [d for flow in flows for d in flow.neighbours()]
    for device in greeted:
        pl.semaphore_signal(barrier, inc=1, device_id=(device,), device_id_type=MESH)
    for load in loads:
        load.wait()

    def rows(start, count):
        return pl.ds(pl.multiple_of(start, count), count)

    def copy(here, there, chunk, send, device):
        part = rows(chunk * SLICE, SLICE)
        return pltpu.make_async_remote_copy(
            src_ref=held.at[here, part],
            dst_ref=held.at[there, part],
            send_sem=send_sem.at[send],
            recv_sem=recv_sem.at[there, chunk],
            device_id=(device,),
            device_id_type=MESH,
        )

    def arrived(buffer, chunk):
        copy(0, buffer, chunk, 0, me).wait_recv()

    pl.semaphore_wait(barrier, len(greeted))

    @pl.loop(0, CHUNKS)
    def _(chunk):
        part = rows(chunk * SLICE, SLICE)
        whole = raw[part, :].astype(jnp.float32)
        norm = jnp.sqrt(jnp.sum(whole * whole, axis=-1, keepdims=True) + 1e-06)
        norms[part, :] = norm
        held[0, part, :] = (whole / norm).astype(jnp.bfloat16)
        for flow in flows:
            there, device = flow.first(chunk)
            copy(0, flow.base + there, chunk, flow.sends, device).start()

    for flow in flows:
        for number, tap in enumerate(getattr(flow, "taps", ())):
            @pl.loop(0, CHUNKS // 2)
            def _(pair, flow=flow, number=number, tap=tap):
                copy(0, flow.base + (1 << tap) - 1, 2 * pair + 1 - flow.side(tap), flow.sends + 4 + number,
                     flow.partner(tap)).start()

    total[...] = jnp.zeros_like(total)
    losses[...] = jnp.zeros_like(losses)

    scale, bias = scale_ref[0], bias_ref[0]
    tasks = agenda(blocks)
    ends = [max(k for k, t in enumerate(tasks) if t[2] == side) for side in range(2)]
    stores = {
        k: pltpu.make_async_copy(total.at[pl.ds(ROWS * k, ROWS)], out, store_sem.at[k])
        for k, out in enumerate((txt_out, img_out))
    }
    where = [0] + [flow.base + buffer for flow, buffer, _ in blocks]
    waits = [0] + [2 if how in ("near", "far") else 1 for _, _, how in blocks]

    def finish(side):
        @pl.loop(0, CHUNKS // 2)
        def _(chunk):
            part = rows(ROWS - ROWS * side + chunk * SLICE, SLICE)
            direction = scale * total[part, :]
            scaled = 1.0 / norms[part, :]
            unit = raw[part, :].astype(jnp.float32) * scaled
            inner = jnp.sum(unit * direction, axis=-1, keepdims=True)
            total[part, :] = (direction - unit * inner) * scaled

        for k, store in stores.items():
            @pl.when(side == 1 - k)
            def _(store=store):
                store.start()

    def pair(task):
        block = pick(task, [t[1] for t in tasks])
        piece = pick(task, [t[2] for t in tasks])
        buffer = pick(block, where)

        @pl.when(pick(block, waits) == 1)
        def _():
            for chunk in range(HALF):
                arrived(buffer, HALF * piece + chunk)

        for number, (flow, _, how) in enumerate(blocks, 1):
            if waits[number] == 2:
                @pl.when(block == number)
                def _(flow=flow, tap=("near", "far").index(how)):
                    for chunk in range(0, HALF, 2):
                        arrived(buffer, HALF * piece + chunk + flow.side(tap))

        side = piece
        mine = rows(ROWS - ROWS * side, ROWS)
        other = held[buffer, rows(piece * PIECE, PIECE), :]
        logits = scale * lax.dot_general(
            held[0, mine, :], other, (((1,), (1,)), ((), ())), preferred_element_type=jnp.float32
        ) + bias
        row = lax.broadcasted_iota(jnp.int32, logits.shape, 0)
        column = lax.broadcasted_iota(jnp.int32, logits.shape, 1)
        diagonal = row == jnp.where(block == 0, column, -1)
        logits = jnp.where(diagonal, -logits, logits)
        small = jnp.exp(-jnp.abs(logits))
        share = 1.0 / (1.0 + small)
        coef = jnp.where(logits >= 0, share, small * share)
        coef = jnp.where(diagonal, -coef, coef)
        loss = jnp.maximum(logits, 0.0) + jnp.log1p(small)
        losses[...] += jnp.where(side == 0, loss, 0.0)
        total[mine, :] += jnp.dot(coef.astype(jnp.bfloat16), other, preferred_element_type=jnp.float32)

        @pl.when((task == ends[0]) | (task == ends[1]))
        def _():
            finish(side)

    due = [sum(t[0] < step for t in tasks) for step in range(STEPS + 2)]

    @pl.loop(0, STEPS + 1)
    def _(step):
        phase = div(step, CHUNKS) + 1
        chunk = rem(step, CHUNKS)
        for flow in flows:
            if flow.phases:
                @pl.when(phase <= flow.phases)
                def _(flow=flow):
                    here, there, device = flow.hop(phase, chunk)
                    arrived(flow.base + here, chunk)
                    copy(flow.base + here, flow.base + there, chunk, flow.sends + phase, device).start()

        @pl.loop(pick(step, due), pick(step + 1, due))
        def _(task):
            pair(task)

    loss_out[...] = jnp.sum(losses[...].T, axis=0, keepdims=True)
    for flow in flows:
        for phase in range(flow.phases + 1):
            pltpu.make_async_remote_copy(
                src_ref=held.at[0], dst_ref=held.at[flow.base], send_sem=send_sem.at[flow.sends + phase],
                recv_sem=recv_sem.at[flow.base, 0], device_id=(me,), device_id_type=MESH,
            ).wait_send()
        for number in range(len(getattr(flow, "taps", ()))):
            pltpu.make_async_remote_copy(
                src_ref=held.at[0, pl.ds(0, ROWS)], dst_ref=held.at[flow.base, pl.ds(0, ROWS)],
                send_sem=send_sem.at[flow.sends + 4 + number], recv_sem=recv_sem.at[flow.base, 0],
                device_id=(me,), device_id_type=MESH,
            ).wait_send()
    for store in stores.values():
        store.wait()


def hand_over(*refs):
    count = (len(refs) - 1) // 2
    copies = [pltpu.make_async_copy(refs[k], refs[count + k], refs[-1].at[k]) for k in range(count)]
    for copy in copies:
        copy.start()
    for copy in copies:
        copy.wait()


def moved(arrays):
    return pl.pallas_call(
        hand_over,
        out_shape=tuple(jax.ShapeDtypeStruct(a.shape, a.dtype) for a in arrays),
        in_specs=[pl.BlockSpec(memory_space=pl.ANY)] * len(arrays),
        out_specs=tuple(pl.BlockSpec(memory_space=pl.ANY) for _ in arrays),
        scratch_shapes=[pltpu.SemaphoreType.DMA((len(arrays),))],
        name="moved",
    )(*arrays)


def window(number, image, text, scale, bias):
    bits = (*WINDOWS[number], TOP_BIT)
    flows, _ = routes(bits)
    buffers = 1 + sum(flow.buffers for flow in flows)
    width = image.shape[1]
    any_space = pl.BlockSpec(memory_space=pl.ANY)
    scalar = pl.BlockSpec(memory_space=pltpu.SMEM)
    return pl.pallas_call(
        functools.partial(kernel, bits),
        out_shape=(
            jax.ShapeDtypeStruct((1, ROWS), jnp.float32),
            jax.ShapeDtypeStruct((ROWS, width), jnp.float32),
            jax.ShapeDtypeStruct((ROWS, width), jnp.float32),
        ),
        in_specs=[any_space, any_space, scalar, scalar],
        out_specs=(pl.BlockSpec(memory_space=pltpu.VMEM), any_space, any_space),
        scratch_shapes=[
            pltpu.VMEM((BOTH, width), jnp.bfloat16),
            pltpu.VMEM((BOTH, 1), jnp.float32),
            pltpu.VMEM((buffers, BOTH, width), jnp.bfloat16),
            pltpu.VMEM((BOTH, width), jnp.float32),
            pltpu.VMEM((ROWS, ROWS), jnp.float32),
            pltpu.SemaphoreType.DMA((2,)),
            pltpu.SemaphoreType.DMA((2,)),
            pltpu.SemaphoreType.DMA((6 * len(flows),)),
            pltpu.SemaphoreType.DMA((buffers, CHUNKS)),
        ],
        compiler_params=pltpu.CompilerParams(
            collective_id=number, has_side_effects=True, vmem_limit_bytes=24 << 20
        ),
        name="window",
    )(image, text, scale, bias)


def per_device(image, text, plan, offset, logit_scale, logit_bias):
    listed = jnp.arange(plan.shape[0], dtype=jnp.int32) - offset[0]
    others = jnp.sum(jnp.where((listed >= 0) & (listed < ROUNDS), plan[:, 0], 0)) - (1 << TOP_BIT)
    high = 31 - lax.clz(others)
    low = 31 - lax.clz(others - jnp.left_shift(jnp.int32(1), high))
    number = lax.shift_right_logical(high * (high - 1), jnp.int32(1)) + low
    branches = [functools.partial(window, k) for k in range(len(WINDOWS))]
    results = lax.switch(number, branches, image, text, logit_scale, logit_bias)
    losses, image_grad, text_grad = moved(results)
    return losses.reshape(ROWS), image_grad, text_grad


def solution(mesh):
    in_specs = (P("dp", None), P("dp", None), P(), P(), P(), P())
    out_specs = (P("dp"), P("dp", None), P("dp", None))
    return jax.shard_map(
        per_device, mesh=mesh, in_specs=in_specs, out_specs=out_specs, check_vma=False
    )
```

```python
import functools

import jax
import jax.numpy as jnp
from jax import lax
from jax.experimental import pallas as pl
from jax.experimental.pallas import tpu as pltpu
from jax.sharding import PartitionSpec as P

MESH = pl.DeviceIdType.MESH
ROUNDS = 3
ROWS = 128
BOTH = 2 * ROWS
CHUNKS = 8
SLICE = BOTH // CHUNKS
PIECE = ROWS
PIECES = BOTH // PIECE
HALF = CHUNKS // 2
STEPS = 3 * CHUNKS
TOP_BIT = 8
RINGS = ((6, 3), (1, 3), (4, 2))
WINDOWS = tuple((low, high) for high in range(TOP_BIT) for low in range(high))


def div(a, b):
    return lax.div(a, jnp.int32(b))


def rem(a, b):
    return lax.rem(a, jnp.int32(b))


def pick(index, table):
    value = jnp.int32(table[0])
    for k in range(1, len(table)):
        if table[k] != table[k - 1]:
            value = jnp.where(index >= k, jnp.int32(table[k]), value)
    return value


class Direct:
    buffers = 1
    phases = 0
    final = 0

    def __init__(self, bit):
        self.bit = bit

    def place(self, me):
        mask = 1 << self.bit
        self.partner = me + (1 - 2 * rem(div(me, mask), 2)) * mask

    def neighbours(self):
        return [self.partner]

    def first(self, chunk):
        return 0, self.partner


class Relay:
    size = 8
    phases = 3
    final = 3

    def __init__(self, bit, taps):
        self.bit = bit
        self.taps = taps
        self.buffers = 4 + len(taps)

    def place(self, me):
        self.me = me
        self.at = rem(div(me, 1 << self.bit), self.size)

    def device(self, step):
        return self.me + (rem(self.at + step + self.size, self.size) - self.at) * (1 << self.bit)

    def side(self, tap):
        return rem(div(self.at, 1 << tap), 2)

    def partner(self, tap):
        return self.me + (1 - 2 * self.side(tap)) * (1 << (self.bit + tap))

    def neighbours(self):
        return [self.device(1), self.device(-1)] + [self.partner(tap) for tap in self.taps if tap]

    def slot(self, hop, down, at):
        buffer = hop - 1
        for number, tap in enumerate(self.taps):
            other = (hop == 1 << tap) & (down == rem(div(at, 1 << tap), 2))
            buffer = jnp.where(other, 4 + number, buffer)
        return buffer

    def hop(self, phase, chunk):
        down = rem(chunk, 2)
        step = 1 - 2 * down
        there = rem(self.at + step + self.size, self.size)
        return self.slot(phase, down, self.at), self.slot(phase + 1, down, there), self.device(step)

    def first(self, chunk):
        _, there, device = self.hop(0, chunk)
        return there, device


def routes(bits):
    flows, blocks = [], []

    def direct(bit, how):
        flows.append(Direct(bit))
        blocks.append((flows[-1], 0, how))

    for first, count in RINGS:
        held = tuple(b - first for b in bits if first <= b < first + count)
        if count == 3 and 2 in held:
            flow = Relay(first, held[:-1])
            flows.append(flow)
            blocks.append((flow, flow.final, "last" if first + 2 == TOP_BIT else "late"))
            for tap in flow.taps:
                blocks.append((flow, (1 << tap) - 1, ("near", "far")[tap]))
        else:
            for low in held:
                direct(first + low, "late" if 1 in held and (count == 3 or len(held) == 2) else "early")
    if 0 in bits:
        direct(0, "early")
    return flows, blocks


def agenda(blocks):
    tasks = [(1 + 2 * piece, 0, piece) for piece in range(PIECES)]
    early = 0
    for number, (flow, _, how) in enumerate(blocks, 1):
        if how == "early":
            steps = (16 + 4 * early, 18 + 4 * early)
            early += 1
        else:
            steps = (24 if flow.phases else 22, 24)
        tasks += [(step, number, piece) for piece, step in enumerate(steps)]
    order = ("near", "late", "far", "last")

    def key(task):
        step, block, piece = task
        if step < STEPS:
            return step, piece, 0
        how = blocks[block - 1][2]
        return step, piece if how in ("late", "last") else 0, order.index(how)

    return sorted(tasks, key=key)


def kernel(bits, img_hbm, txt_hbm, scale_ref, bias_ref, loss_out, img_out, txt_out,
           raw, norms, held, total, losses, load_sem, store_sem, send_sem, recv_sem, ready_sem):
    me = lax.axis_index("dp")
    flows, blocks = routes(bits)
    base = 1
    for number, flow in enumerate(flows):
        flow.place(me)
        flow.base, flow.sends = base, 6 * number
        base += flow.buffers

    loads = [
        pltpu.make_async_copy(src, raw.at[pl.ds(ROWS * k, ROWS)], load_sem.at[k])
        for k, src in enumerate((txt_hbm, img_hbm))
    ]
    for load in loads:
        load.start()
    barrier = pltpu.get_barrier_semaphore()
    greeted = [d for flow in flows for d in flow.neighbours()]
    far = next(flow for flow, _, how in blocks if how == "last")
    early_edge = (far.at == 0) | (far.at == 3)
    late_edge = (far.at == 4) | (far.at == 7)
    over = far.device(jnp.where((far.at == 0) | (far.at == 4), -1, 1))
    for device in greeted:
        @pl.when(jnp.logical_not(late_edge & (device == over)))
        def _(device=device):
            pl.semaphore_signal(barrier, inc=1, device_id=(device,), device_id_type=MESH)
    for load in loads:
        load.wait()

    def rows(start, count):
        return pl.ds(pl.multiple_of(start, count), count)

    def copy(here, there, chunk, send, device):
        part = rows(chunk * SLICE, SLICE)
        return pltpu.make_async_remote_copy(
            src_ref=held.at[here, part],
            dst_ref=held.at[there, part],
            send_sem=send_sem.at[send],
            recv_sem=recv_sem.at[there, chunk],
            device_id=(device,),
            device_id_type=MESH,
        )

    def arrived(buffer, chunk):
        copy(0, buffer, chunk, 0, me).wait_recv()

    pl.semaphore_wait(barrier, len(greeted) - early_edge.astype(jnp.int32))

    @pl.when(late_edge)
    def _():
        pl.semaphore_signal(ready_sem, inc=1, device_id=(over,), device_id_type=MESH)

    @pl.loop(0, CHUNKS)
    def _(chunk):
        part = rows(chunk * SLICE, SLICE)
        whole = raw[part, :].astype(jnp.float32)
        norm = jnp.sqrt(jnp.sum(whole * whole, axis=-1, keepdims=True) + 1e-06)
        norms[part, :] = norm
        held[0, part, :] = (whole / norm).astype(jnp.bfloat16)
        for flow in flows:
            there, device = flow.first(chunk)
            if flow is far:
                @pl.when(jnp.logical_not(early_edge & (device == over)))
                def _(there=there, device=device):
                    copy(0, far.base + there, chunk, far.sends, device).start()
            else:
                copy(0, flow.base + there, chunk, flow.sends, device).start()

    def send_rest(flow):
        @pl.loop(0, HALF)
        def _(two):
            for number, tap in enumerate(flow.taps):
                copy(0, flow.base + (1 << tap) - 1, 2 * two + 1 - flow.side(tap), flow.sends + 4 + number,
                     flow.partner(tap)).start()

    put_off = far.taps == (0,)
    soon = far.at < 4
    for flow in flows:
        if flow.phases and flow.taps:
            if flow is far and put_off:
                @pl.when(soon)
                def _():
                    send_rest(far)
            else:
                send_rest(flow)

    @pl.when(early_edge)
    def _():
        pl.semaphore_wait(ready_sem, 1)

        @pl.loop(0, HALF)
        def _(two):
            chunk = 2 * two + (far.at == 0).astype(jnp.int32)
            there, _ = far.first(chunk)
            copy(0, far.base + there, chunk, far.sends, over).start()

    total[...] = jnp.zeros_like(total)
    losses[...] = jnp.zeros_like(losses)

    scale, bias = scale_ref[0], bias_ref[0]
    tasks = agenda(blocks)
    ends = [max(k for k, t in enumerate(tasks) if t[2] == side) for side in range(2)]
    stores = {
        k: pltpu.make_async_copy(total.at[pl.ds(ROWS * k, ROWS)], out, store_sem.at[k])
        for k, out in enumerate((txt_out, img_out))
    }
    where = [0] + [flow.base + buffer for flow, buffer, _ in blocks]
    waits = [0] + [2 if how in ("near", "far") else 1 for _, _, how in blocks]

    def finish(side):
        @pl.loop(0, CHUNKS // 2)
        def _(chunk):
            part = rows(ROWS - ROWS * side + chunk * SLICE, SLICE)
            direction = scale * total[part, :]
            scaled = 1.0 / norms[part, :]
            unit = raw[part, :].astype(jnp.float32) * scaled
            inner = jnp.sum(unit * direction, axis=-1, keepdims=True)
            total[part, :] = (direction - unit * inner) * scaled

        for k, store in stores.items():
            @pl.when(side == 1 - k)
            def _(store=store):
                store.start()

    def pair(task):
        block = pick(task, [t[1] for t in tasks])
        piece = pick(task, [t[2] for t in tasks])
        buffer = pick(block, where)

        @pl.when(pick(block, waits) == 1)
        def _():
            for chunk in range(HALF):
                arrived(buffer, HALF * piece + chunk)

        for number, (flow, _, how) in enumerate(blocks, 1):
            if waits[number] == 2:
                @pl.when(block == number)
                def _(flow=flow, tap=("near", "far").index(how)):
                    for chunk in range(0, HALF, 2):
                        arrived(buffer, HALF * piece + chunk + flow.side(tap))

        side = piece
        mine = rows(ROWS - ROWS * side, ROWS)
        other = held[buffer, rows(piece * PIECE, PIECE), :]
        logits = scale * lax.dot_general(
            held[0, mine, :], other, (((1,), (1,)), ((), ())), preferred_element_type=jnp.float32
        ) + bias
        row = lax.broadcasted_iota(jnp.int32, logits.shape, 0)
        column = lax.broadcasted_iota(jnp.int32, logits.shape, 1)
        diagonal = row == jnp.where(block == 0, column, -1)
        logits = jnp.where(diagonal, -logits, logits)
        small = jnp.exp(-jnp.abs(logits))
        share = 1.0 / (1.0 + small)
        coef = jnp.where(logits >= 0, share, small * share)
        coef = jnp.where(diagonal, -coef, coef)
        loss = jnp.maximum(logits, 0.0) + jnp.log1p(small)
        losses[...] += jnp.where(side == 0, loss, 0.0)
        total[mine, :] += jnp.dot(coef.astype(jnp.bfloat16), other, preferred_element_type=jnp.float32)

        @pl.when((task == ends[0]) | (task == ends[1]))
        def _():
            finish(side)

    due = [sum(t[0] < step for t in tasks) for step in range(STEPS + 2)]

    @pl.loop(0, STEPS + 1)
    def _(step):
        phase = div(step, CHUNKS) + 1
        chunk = rem(step, CHUNKS)
        for flow in flows:
            if flow.phases:
                @pl.when(phase <= flow.phases)
                def _(flow=flow):
                    here, there, device = flow.hop(phase, chunk)
                    arrived(flow.base + here, chunk)
                    copy(flow.base + here, flow.base + there, chunk, flow.sends + phase, device).start()

        if put_off:
            @pl.when((step == STEPS - 1) & jnp.logical_not(soon))
            def _():
                send_rest(far)

        @pl.loop(pick(step, due), pick(step + 1, due))
        def _(task):
            pair(task)

    loss_out[...] = jnp.sum(losses[...].T, axis=0, keepdims=True)
    for flow in flows:
        for phase in range(flow.phases + 1):
            pltpu.make_async_remote_copy(
                src_ref=held.at[0], dst_ref=held.at[flow.base], send_sem=send_sem.at[flow.sends + phase],
                recv_sem=recv_sem.at[flow.base, 0], device_id=(me,), device_id_type=MESH,
            ).wait_send()
        for number in range(len(getattr(flow, "taps", ()))):
            pltpu.make_async_remote_copy(
                src_ref=held.at[0, pl.ds(0, ROWS)], dst_ref=held.at[flow.base, pl.ds(0, ROWS)],
                send_sem=send_sem.at[flow.sends + 4 + number], recv_sem=recv_sem.at[flow.base, 0],
                device_id=(me,), device_id_type=MESH,
            ).wait_send()
    for store in stores.values():
        store.wait()


def hand_over(*refs):
    count = (len(refs) - 1) // 2
    copies = [pltpu.make_async_copy(refs[k], refs[count + k], refs[-1].at[k]) for k in range(count)]
    for copy in copies:
        copy.start()
    for copy in copies:
        copy.wait()


def moved(arrays):
    return pl.pallas_call(
        hand_over,
        out_shape=tuple(jax.ShapeDtypeStruct(a.shape, a.dtype) for a in arrays),
        in_specs=[pl.BlockSpec(memory_space=pl.ANY)] * len(arrays),
        out_specs=tuple(pl.BlockSpec(memory_space=pl.ANY) for _ in arrays),
        scratch_shapes=[pltpu.SemaphoreType.DMA((len(arrays),))],
        name="moved",
    )(*arrays)


def window(number, image, text, scale, bias):
    bits = (*WINDOWS[number], TOP_BIT)
    flows, _ = routes(bits)
    buffers = 1 + sum(flow.buffers for flow in flows)
    width = image.shape[1]
    any_space = pl.BlockSpec(memory_space=pl.ANY)
    scalar = pl.BlockSpec(memory_space=pltpu.SMEM)
    return pl.pallas_call(
        functools.partial(kernel, bits),
        out_shape=(
            jax.ShapeDtypeStruct((1, ROWS), jnp.float32),
            jax.ShapeDtypeStruct((ROWS, width), jnp.float32),
            jax.ShapeDtypeStruct((ROWS, width), jnp.float32),
        ),
        in_specs=[any_space, any_space, scalar, scalar],
        out_specs=(pl.BlockSpec(memory_space=pltpu.VMEM), any_space, any_space),
        scratch_shapes=[
            pltpu.VMEM((BOTH, width), jnp.bfloat16),
            pltpu.VMEM((BOTH, 1), jnp.float32),
            pltpu.VMEM((buffers, BOTH, width), jnp.bfloat16),
            pltpu.VMEM((BOTH, width), jnp.float32),
            pltpu.VMEM((ROWS, ROWS), jnp.float32),
            pltpu.SemaphoreType.DMA((2,)),
            pltpu.SemaphoreType.DMA((2,)),
            pltpu.SemaphoreType.DMA((6 * len(flows),)),
            pltpu.SemaphoreType.DMA((buffers, CHUNKS)),
            pltpu.SemaphoreType.REGULAR,
        ],
        compiler_params=pltpu.CompilerParams(
            collective_id=number, has_side_effects=True, vmem_limit_bytes=24 << 20
        ),
        name="window",
    )(image, text, scale, bias)


def per_device(image, text, plan, offset, logit_scale, logit_bias):
    listed = jnp.arange(plan.shape[0], dtype=jnp.int32) - offset[0]
    others = jnp.sum(jnp.where((listed >= 0) & (listed < ROUNDS), plan[:, 0], 0)) - (1 << TOP_BIT)
    high = 31 - lax.clz(others)
    low = 31 - lax.clz(others - jnp.left_shift(jnp.int32(1), high))
    number = lax.shift_right_logical(high * (high - 1), jnp.int32(1)) + low
    branches = [functools.partial(window, k) for k in range(len(WINDOWS))]
    results = lax.switch(number, branches, image, text, logit_scale, logit_bias)
    losses, image_grad, text_grad = moved(results)
    return losses.reshape(ROWS), image_grad, text_grad


def solution(mesh):
    in_specs = (P("dp", None), P("dp", None), P(), P(), P(), P())
    out_specs = (P("dp"), P("dp", None), P("dp", None))
    return jax.shard_map(
        per_device, mesh=mesh, in_specs=in_specs, out_specs=out_specs, check_vma=False
    )
```

```python
import functools

import jax
import jax.numpy as jnp
from jax import lax
from jax.experimental import pallas as pl
from jax.experimental.pallas import tpu as pltpu
from jax.sharding import PartitionSpec as P

MESH = pl.DeviceIdType.MESH
ROUNDS = 3
ROWS = 128
BOTH = 2 * ROWS
CHUNKS = 8
SLICE = BOTH // CHUNKS
PIECE = ROWS
PIECES = BOTH // PIECE
HALF = CHUNKS // 2
STEPS = 3 * CHUNKS
TOP_BIT = 8
RINGS = ((6, 3), (1, 3), (4, 2))
WINDOWS = tuple((low, high) for high in range(TOP_BIT) for low in range(high))


def div(a, b):
    return lax.div(a, jnp.int32(b))


def rem(a, b):
    return lax.rem(a, jnp.int32(b))


def pick(index, table):
    value = jnp.int32(table[0])
    for k in range(1, len(table)):
        if table[k] != table[k - 1]:
            value = jnp.where(index >= k, jnp.int32(table[k]), value)
    return value


class Direct:
    buffers = 1
    phases = 0
    final = 0

    def __init__(self, bit):
        self.bit = bit

    def place(self, me):
        mask = 1 << self.bit
        self.partner = me + (1 - 2 * rem(div(me, mask), 2)) * mask

    def neighbours(self):
        return [self.partner]

    def first(self, chunk):
        return 0, self.partner


class Relay:
    size = 8
    phases = 3
    final = 3

    def __init__(self, bit, taps, turned):
        self.bit = bit
        self.taps = taps
        self.turned = turned and not taps
        self.buffers = 4 + len(taps) + self.turned

    def place(self, me):
        self.me = me
        self.at = rem(div(me, 1 << self.bit), self.size)

    def device(self, step):
        return self.me + (rem(self.at + step + self.size, self.size) - self.at) * (1 << self.bit)

    def side(self, tap):
        return rem(div(self.at, 1 << tap), 2)

    def partner(self, tap):
        return self.me + (1 - 2 * self.side(tap)) * (1 << (self.bit + tap))

    def neighbours(self):
        return [self.device(1), self.device(-1)] + [self.partner(tap) for tap in self.taps if tap]

    def slot(self, hop, down, at):
        buffer = hop - 1
        for number, tap in enumerate(self.taps):
            other = (hop == 1 << tap) & (down == rem(div(at, 1 << tap), 2))
            buffer = jnp.where(other, 4 + number, buffer)
        return buffer

    def hop(self, phase, chunk):
        down = rem(chunk, 2)
        step = 1 - 2 * down
        there = rem(self.at + step + self.size, self.size)
        return self.slot(phase, down, self.at), self.slot(phase + 1, down, there), self.device(step)

    def first(self, chunk):
        _, there, device = self.hop(0, chunk)
        if self.turned:
            down = self.turns(chunk) & (self.at == 4)
            there = jnp.where(down, 4, there)
            device = jnp.where(down, self.device(-1), device)
        return there, device

    def turns(self, chunk):
        return (chunk == 0) | (chunk == 2)


def routes(bits):
    flows, blocks = [], []

    def direct(bit, how):
        flows.append(Direct(bit))
        blocks.append((flows[-1], 0, how))

    for first, count in RINGS:
        held = tuple(b - first for b in bits if first <= b < first + count)
        if count == 3 and 2 in held:
            flow = Relay(first, held[:-1], first + 2 == TOP_BIT)
            flows.append(flow)
            blocks.append((flow, flow.final, "last" if first + 2 == TOP_BIT else "late"))
            for tap in flow.taps:
                blocks.append((flow, (1 << tap) - 1, ("near", "far")[tap]))
        else:
            for low in held:
                direct(first + low, "late" if 1 in held and (count == 3 or len(held) == 2) else "early")
    if 0 in bits:
        direct(0, "early")
    return flows, blocks


def agenda(blocks):
    tasks = [(1 + 2 * piece, 0, piece) for piece in range(PIECES)]
    early = 0
    for number, (flow, _, how) in enumerate(blocks, 1):
        if how == "early":
            steps = (16 + 4 * early, 18 + 4 * early)
            early += 1
        else:
            steps = (24 if flow.phases else 22, 24)
        tasks += [(step, number, piece) for piece, step in enumerate(steps)]
    order = ("near", "late", "far", "last")

    def key(task):
        step, block, piece = task
        if step < STEPS:
            return step, piece, 0
        how = blocks[block - 1][2]
        return step, piece if how in ("late", "last") else 0, order.index(how)

    return sorted(tasks, key=key)


def kernel(bits, img_hbm, txt_hbm, scale_ref, bias_ref, loss_out, total,
           raw, norms, held, losses, load_sem, send_sem, recv_sem, ready_sem):
    me = lax.axis_index("dp")
    flows, blocks = routes(bits)
    base = 1
    for number, flow in enumerate(flows):
        flow.place(me)
        flow.base, flow.sends = base, 6 * number
        base += flow.buffers

    loads = [
        pltpu.make_async_copy(src, raw.at[pl.ds(ROWS * k, ROWS)], load_sem.at[k])
        for k, src in enumerate((txt_hbm, img_hbm))
    ]
    for load in loads:
        load.start()
    barrier = pltpu.get_barrier_semaphore()
    greeted = [d for flow in flows for d in flow.neighbours()]
    far = next(flow for flow, _, how in blocks if how == "last")
    early_edge = (far.at == 0) | (far.at == 3)
    late_edge = (far.at == 4) | (far.at == 7)
    over = far.device(jnp.where((far.at == 0) | (far.at == 4), -1, 1))
    for device in greeted:
        @pl.when(jnp.logical_not(late_edge & (device == over)))
        def _(device=device):
            pl.semaphore_signal(barrier, inc=1, device_id=(device,), device_id_type=MESH)
    for load in loads:
        load.wait()

    def rows(start, count):
        return pl.ds(pl.multiple_of(start, count), count)

    def copy(here, there, chunk, send, device):
        part = rows(chunk * SLICE, SLICE)
        return pltpu.make_async_remote_copy(
            src_ref=held.at[here, part],
            dst_ref=held.at[there, part],
            send_sem=send_sem.at[send],
            recv_sem=recv_sem.at[there, chunk],
            device_id=(device,),
            device_id_type=MESH,
        )

    def arrived(buffer, chunk):
        copy(0, buffer, chunk, 0, me).wait_recv()

    pl.semaphore_wait(barrier, len(greeted) - early_edge.astype(jnp.int32))

    @pl.when(late_edge)
    def _():
        pl.semaphore_signal(ready_sem, inc=1, device_id=(over,), device_id_type=MESH)

    @pl.loop(0, CHUNKS)
    def _(chunk):
        part = rows(chunk * SLICE, SLICE)
        whole = raw[part, :].astype(jnp.float32)
        norm = jnp.sqrt(jnp.sum(whole * whole, axis=-1, keepdims=True) + 1e-06)
        norms[part, :] = norm
        held[0, part, :] = (whole / norm).astype(jnp.bfloat16)
        for flow in flows:
            there, device = flow.first(chunk)
            if flow is far:
                @pl.when(jnp.logical_not(early_edge & (device == over)))
                def _(there=there, device=device):
                    copy(0, far.base + there, chunk, far.sends, device).start()
            else:
                copy(0, flow.base + there, chunk, flow.sends, device).start()

    def send_rest(flow):
        @pl.loop(0, HALF)
        def _(two):
            for number, tap in enumerate(flow.taps):
                copy(0, flow.base + (1 << tap) - 1, 2 * two + 1 - flow.side(tap), flow.sends + 4 + number,
                     flow.partner(tap)).start()

    put_off = far.taps == (0,)
    soon = far.at < 4
    for flow in flows:
        if flow.phases and flow.taps:
            if flow is far and put_off:
                @pl.when(soon)
                def _():
                    send_rest(far)
            else:
                send_rest(flow)

    @pl.when(early_edge)
    def _():
        pl.semaphore_wait(ready_sem, 1)

        @pl.loop(0, HALF)
        def _(two):
            chunk = 2 * two + (far.at == 0).astype(jnp.int32)
            there, _ = far.first(chunk)
            copy(0, far.base + there, chunk, far.sends, over).start()

    total[...] = jnp.zeros_like(total)
    losses[...] = jnp.zeros_like(losses)

    scale, bias = scale_ref[0], bias_ref[0]
    tasks = agenda(blocks)
    ends = [max(k for k, t in enumerate(tasks) if t[2] == side) for side in range(2)]
    where = [0] + [flow.base + buffer for flow, buffer, _ in blocks]
    waits = [0] + [2 if how in ("near", "far") else 1 for _, _, how in blocks]

    def finish(side):
        @pl.loop(0, CHUNKS // 2)
        def _(chunk):
            part = rows(ROWS - ROWS * side + chunk * SLICE, SLICE)
            direction = scale * total[part, :]
            scaled = 1.0 / norms[part, :]
            unit = raw[part, :].astype(jnp.float32) * scaled
            inner = jnp.sum(unit * direction, axis=-1, keepdims=True)
            total[part, :] = (direction - unit * inner) * scaled

    def pair(task):
        block = pick(task, [t[1] for t in tasks])
        piece = pick(task, [t[2] for t in tasks])
        buffer = pick(block, where)

        @pl.when(pick(block, waits) == 1)
        def _():
            for chunk in range(HALF):
                arrived(buffer, HALF * piece + chunk)

        for number, (flow, _, how) in enumerate(blocks, 1):
            if waits[number] == 2:
                @pl.when(block == number)
                def _(flow=flow, tap=("near", "far").index(how)):
                    for chunk in range(0, HALF, 2):
                        arrived(buffer, HALF * piece + chunk + flow.side(tap))

        side = piece
        mine = rows(ROWS - ROWS * side, ROWS)
        other = held[buffer, rows(piece * PIECE, PIECE), :]
        logits = scale * lax.dot_general(
            held[0, mine, :], other, (((1,), (1,)), ((), ())), preferred_element_type=jnp.float32
        ) + bias
        row = lax.broadcasted_iota(jnp.int32, logits.shape, 0)
        column = lax.broadcasted_iota(jnp.int32, logits.shape, 1)
        diagonal = row == jnp.where(block == 0, column, -1)
        logits = jnp.where(diagonal, -logits, logits)
        small = jnp.exp(-jnp.abs(logits))
        share = 1.0 / (1.0 + small)
        coef = jnp.where(logits >= 0, share, small * share)
        coef = jnp.where(diagonal, -coef, coef)
        loss = jnp.maximum(logits, 0.0) + jnp.log1p(small)
        losses[...] += jnp.where(side == 0, loss, 0.0)
        total[mine, :] += jnp.dot(coef.astype(jnp.bfloat16), other, preferred_element_type=jnp.float32)

        @pl.when((task == ends[0]) | (task == ends[1]))
        def _():
            finish(side)

    due = [sum(t[0] < step for t in tasks) for step in range(STEPS + 2)]

    @pl.loop(0, STEPS + 1)
    def _(step):
        phase = div(step, CHUNKS) + 1
        chunk = rem(step, CHUNKS)
        for flow in flows:
            if flow.phases:
                here_too = phase <= flow.phases
                if flow.turned:
                    @pl.when(here_too & flow.turns(chunk) & (flow.at == 4 - phase))
                    def _(flow=flow):
                        arrived(flow.base + 4, chunk)
                        there = jnp.where(phase == 3, flow.final, 4)
                        copy(flow.base + 4, flow.base + there, chunk, flow.sends + 4, flow.device(-1)).start()

                    here_too &= jnp.logical_not(flow.turns(chunk) & (flow.at == 4 + phase))

                @pl.when(here_too)
                def _(flow=flow):
                    here, there, device = flow.hop(phase, chunk)
                    arrived(flow.base + here, chunk)
                    copy(flow.base + here, flow.base + there, chunk, flow.sends + phase, device).start()

        if put_off:
            @pl.when((step == STEPS - 1) & jnp.logical_not(soon))
            def _():
                send_rest(far)

        @pl.loop(pick(step, due), pick(step + 1, due))
        def _(task):
            pair(task)

    loss_out[...] = jnp.sum(losses[...].T, axis=0, keepdims=True)
    def sent(send, count):
        part = pl.ds(0, count)
        pltpu.make_async_remote_copy(
            src_ref=held.at[0, part], dst_ref=held.at[1, part], send_sem=send_sem.at[send],
            recv_sem=recv_sem.at[1, 0], device_id=(me,), device_id_type=MESH,
        ).wait_send()

    for flow in flows:
        for phase in range(flow.phases + 1):
            if phase and flow.turned:
                @pl.when(flow.at == 4 + phase)
                def _(flow=flow, phase=phase):
                    sent(flow.sends + phase, BOTH - 2 * SLICE)

                @pl.when(flow.at != 4 + phase)
                def _(flow=flow, phase=phase):
                    sent(flow.sends + phase, BOTH)
            else:
                sent(flow.sends + phase, BOTH)
        for number in range(len(getattr(flow, "taps", ()))):
            sent(flow.sends + 4 + number, ROWS)
        if flow.phases and flow.turned:
            @pl.when((flow.at > 0) & (flow.at < 4))
            def _(flow=flow):
                sent(flow.sends + 4, 2 * SLICE)


def hand_over(losses, grads, losses_out, image_out, text_out, sems):
    sources = (losses, grads.at[pl.ds(ROWS, ROWS)], grads.at[pl.ds(0, ROWS)])
    places = (losses_out, image_out, text_out)
    copies = [pltpu.make_async_copy(src, dst, sems.at[k]) for k, (src, dst) in enumerate(zip(sources, places))]
    for copy in copies:
        copy.start()
    for copy in copies:
        copy.wait()


def moved(losses, grads):
    half = jax.ShapeDtypeStruct((ROWS, grads.shape[1]), grads.dtype)
    return pl.pallas_call(
        hand_over,
        out_shape=(jax.ShapeDtypeStruct(losses.shape, losses.dtype), half, half),
        in_specs=[pl.BlockSpec(memory_space=pl.ANY)] * 2,
        out_specs=(pl.BlockSpec(memory_space=pl.ANY),) * 3,
        scratch_shapes=[pltpu.SemaphoreType.DMA((3,))],
        name="moved",
    )(losses, grads)


def window(number, image, text, scale, bias):
    bits = (*WINDOWS[number], TOP_BIT)
    flows, _ = routes(bits)
    buffers = 1 + sum(flow.buffers for flow in flows)
    width = image.shape[1]
    any_space = pl.BlockSpec(memory_space=pl.ANY)
    scalar = pl.BlockSpec(memory_space=pltpu.SMEM)
    return pl.pallas_call(
        functools.partial(kernel, bits),
        out_shape=(
            jax.ShapeDtypeStruct((1, ROWS), jnp.float32),
            jax.ShapeDtypeStruct((BOTH, width), jnp.float32),
        ),
        in_specs=[any_space, any_space, scalar, scalar],
        out_specs=(pl.BlockSpec(memory_space=pltpu.VMEM), pl.BlockSpec(memory_space=pltpu.VMEM)),
        scratch_shapes=[
            pltpu.VMEM((BOTH, width), jnp.bfloat16),
            pltpu.VMEM((BOTH, 1), jnp.float32),
            pltpu.VMEM((buffers, BOTH, width), jnp.bfloat16),
            pltpu.VMEM((ROWS, ROWS), jnp.float32),
            pltpu.SemaphoreType.DMA((2,)),
            pltpu.SemaphoreType.DMA((6 * len(flows),)),
            pltpu.SemaphoreType.DMA((buffers, CHUNKS)),
            pltpu.SemaphoreType.REGULAR,
        ],
        compiler_params=pltpu.CompilerParams(
            collective_id=number, has_side_effects=True, vmem_limit_bytes=24 << 20
        ),
        name="window",
    )(image, text, scale, bias)


def per_device(image, text, plan, offset, logit_scale, logit_bias):
    column = plan[:, :1]
    listed = lax.broadcasted_iota(jnp.int32, column.shape, 0) - offset[0]
    others = jnp.sum(jnp.where((listed >= 0) & (listed < ROUNDS), column, 0)) - (1 << TOP_BIT)
    high = 31 - lax.clz(others)
    low = 31 - lax.clz(others - jnp.left_shift(jnp.int32(1), high))
    number = lax.shift_right_logical(high * (high - 1), jnp.int32(1)) + low
    branches = [functools.partial(window, k) for k in range(len(WINDOWS))]
    losses, image_grad, text_grad = moved(
        *lax.switch(number, branches, image, text, logit_scale, logit_bias)
    )
    return losses.reshape(ROWS), image_grad, text_grad


def solution(mesh):
    in_specs = (P("dp", None), P("dp", None), P(), P(), P(), P())
    out_specs = (P("dp"), P("dp", None), P("dp", None))
    return jax.shard_map(
        per_device, mesh=mesh, in_specs=in_specs, out_specs=out_specs, check_vma=False
    )
```

```python
import functools

import jax
import jax.numpy as jnp
from jax import lax
from jax.experimental import pallas as pl
from jax.experimental.pallas import tpu as pltpu
from jax.sharding import PartitionSpec as P

MESH = pl.DeviceIdType.MESH
ROUNDS = 3
ROWS = 128
BOTH = 2 * ROWS
CHUNKS = 8
SLICE = BOTH // CHUNKS
PIECE = ROWS
PIECES = BOTH // PIECE
HALF = CHUNKS // 2
STEPS = 3 * CHUNKS
TURNED = 3
TOP_BIT = 8
RINGS = ((6, 3), (1, 3), (4, 2))
WINDOWS = tuple((low, high) for high in range(TOP_BIT) for low in range(high))


def div(a, b):
    return lax.div(a, jnp.int32(b))


def rem(a, b):
    return lax.rem(a, jnp.int32(b))


def pick(index, table):
    value = jnp.int32(table[0])
    for k in range(1, len(table)):
        if table[k] != table[k - 1]:
            value = jnp.where(index >= k, jnp.int32(table[k]), value)
    return value


class Direct:
    buffers = 1
    phases = 0
    final = 0

    def __init__(self, bit):
        self.bit = bit

    def place(self, me):
        mask = 1 << self.bit
        self.partner = me + (1 - 2 * rem(div(me, mask), 2)) * mask

    def neighbours(self):
        return [self.partner]

    def first(self, chunk):
        return 0, self.partner


class Relay:
    size = 8
    phases = 3
    final = 3

    def __init__(self, bit, taps, turned):
        self.bit = bit
        self.taps = taps
        self.turned = turned and not taps
        self.buffers = 4 + len(taps) + self.turned

    def place(self, me):
        self.me = me
        self.at = rem(div(me, 1 << self.bit), self.size)

    def device(self, step):
        return self.me + (rem(self.at + step + self.size, self.size) - self.at) * (1 << self.bit)

    def side(self, tap):
        return rem(div(self.at, 1 << tap), 2)

    def partner(self, tap):
        return self.me + (1 - 2 * self.side(tap)) * (1 << (self.bit + tap))

    def neighbours(self):
        return [self.device(1), self.device(-1)] + [self.partner(tap) for tap in self.taps if tap]

    def slot(self, hop, down, at):
        buffer = hop - 1
        for number, tap in enumerate(self.taps):
            other = (hop == 1 << tap) & (down == rem(div(at, 1 << tap), 2))
            buffer = jnp.where(other, 4 + number, buffer)
        return buffer

    def hop(self, phase, chunk):
        down = rem(chunk, 2)
        step = 1 - 2 * down
        there = rem(self.at + step + self.size, self.size)
        return self.slot(phase, down, self.at), self.slot(phase + 1, down, there), self.device(step)

    def first(self, chunk):
        _, there, device = self.hop(0, chunk)
        if self.turned:
            down = self.turns(chunk) & (self.at == 4)
            there = jnp.where(down, 4, there)
            device = jnp.where(down, self.device(-1), device)
        return there, device

    def turns(self, chunk):
        return (chunk == 0) | (chunk == 2)


class Pairs(Relay):
    buffers = 7
    final = 5
    turned = False
    taps = ()

    def __init__(self, bit):
        self.bit = bit

    def place(self, me):
        super().place(me)
        self.low = rem(div(self.at, 2), 2)
        self.mid = rem(div(self.at + 1, 2), 2)

    def first(self, chunk):
        return self.low, self.device(1 - 2 * self.low)

    def hop(self, phase, chunk):
        low, mid = self.low, self.mid == 1
        second = phase == 2
        here = jnp.where(
            mid,
            jnp.where(phase == 1, 1 - low, jnp.where(second, low, 2)),
            jnp.where(phase == 1, 2, jnp.where(second, 3 + low, 4 - low)),
        )
        there = jnp.where(mid, jnp.where(phase == 3, 4 - low, 2), jnp.where(phase == 1, 4 - low, 5))
        step = 1 - 2 * low
        return here, there, self.device(jnp.where(second, step, -step))

    def turns(self, chunk):
        return chunk >= CHUNKS - TURNED


def routes(bits):
    flows, blocks = [], []

    def direct(bit, how):
        flows.append(Direct(bit))
        blocks.append((flows[-1], 0, how))

    for first, count in RINGS:
        held = tuple(b - first for b in bits if first <= b < first + count)
        if count == 3 and 2 in held:
            top = first + 2 == TOP_BIT
            paired = top and held == (1, 2)
            flow = Pairs(first) if paired else Relay(first, held[:-1], top)
            flows.append(flow)
            if paired:
                blocks.append((flow, 2, "passed"))
            blocks.append((flow, flow.final, "last" if first + 2 == TOP_BIT else "late"))
            for tap in flow.taps:
                blocks.append((flow, (1 << tap) - 1, ("near", "far")[tap]))
        else:
            for low in held:
                direct(first + low, "late" if 1 in held and (count == 3 or len(held) == 2) else "early")
    if 0 in bits:
        direct(0, "early")
    return flows, blocks


def agenda(blocks):
    tasks = [(1 + 2 * piece, 0, piece) for piece in range(PIECES)]
    early = 0
    for number, (flow, _, how) in enumerate(blocks, 1):
        if how == "early":
            steps = (16 + 4 * early, 18 + 4 * early)
            early += 1
        elif how == "passed":
            steps = (20, 24)
        elif how == "last" and isinstance(flow, Pairs):
            steps = (23, 24)
        else:
            steps = (24 if flow.phases else 22, 24)
        tasks += [(step, number, piece) for piece, step in enumerate(steps)]
    order = ("passed", "near", "late", "far", "last")

    def key(task):
        step, block, piece = task
        if step < STEPS:
            return step, piece, 0
        how = blocks[block - 1][2]
        return step, piece if how in ("late", "last") else 0, order.index(how)

    return sorted(tasks, key=key)


def kernel(bits, img_hbm, txt_hbm, scale_ref, bias_ref, loss_out, total,
           raw, norms, held, losses, load_sem, send_sem, recv_sem, ready_sem):
    me = lax.axis_index("dp")
    flows, blocks = routes(bits)
    base = 1
    for number, flow in enumerate(flows):
        flow.place(me)
        flow.base, flow.sends = base, 6 * number
        base += flow.buffers

    loads = [
        pltpu.make_async_copy(src, raw.at[pl.ds(ROWS * k, ROWS)], load_sem.at[k])
        for k, src in enumerate((txt_hbm, img_hbm))
    ]
    for load in loads:
        load.start()
    barrier = pltpu.get_barrier_semaphore()
    greeted = [d for flow in flows for d in flow.neighbours()]
    far = next(flow for flow, _, how in blocks if how == "last")
    early_edge = (far.at == 0) | (far.at == 3)
    late_edge = (far.at == 4) | (far.at == 7)
    over = far.device(jnp.where((far.at == 0) | (far.at == 4), -1, 1))
    for device in greeted:
        @pl.when(jnp.logical_not(late_edge & (device == over)))
        def _(device=device):
            pl.semaphore_signal(barrier, inc=1, device_id=(device,), device_id_type=MESH)
    for load in loads:
        load.wait()

    def rows(start, count):
        return pl.ds(pl.multiple_of(start, count), count)

    def copy(here, there, chunk, send, device):
        part = rows(chunk * SLICE, SLICE)
        return pltpu.make_async_remote_copy(
            src_ref=held.at[here, part],
            dst_ref=held.at[there, part],
            send_sem=send_sem.at[send],
            recv_sem=recv_sem.at[there, chunk],
            device_id=(device,),
            device_id_type=MESH,
        )

    def arrived(buffer, chunk):
        copy(0, buffer, chunk, 0, me).wait_recv()

    pl.semaphore_wait(barrier, len(greeted) - early_edge.astype(jnp.int32))

    @pl.when(late_edge)
    def _():
        pl.semaphore_signal(ready_sem, inc=1, device_id=(over,), device_id_type=MESH)

    @pl.loop(0, CHUNKS)
    def _(chunk):
        part = rows(chunk * SLICE, SLICE)
        whole = raw[part, :].astype(jnp.float32)
        norm = jnp.sqrt(jnp.sum(whole * whole, axis=-1, keepdims=True) + 1e-06)
        norms[part, :] = norm
        held[0, part, :] = (whole / norm).astype(jnp.bfloat16)
        for flow in flows:
            there, device = flow.first(chunk)
            if flow is far:
                @pl.when(jnp.logical_not(early_edge & (device == over)))
                def _(there=there, device=device):
                    copy(0, far.base + there, chunk, far.sends, device).start()
            else:
                copy(0, flow.base + there, chunk, flow.sends, device).start()

    def send_rest(flow):
        @pl.loop(0, HALF)
        def _(two):
            for number, tap in enumerate(flow.taps):
                copy(0, flow.base + (1 << tap) - 1, 2 * two + 1 - flow.side(tap), flow.sends + 4 + number,
                     flow.partner(tap)).start()

    put_off = far.taps == (0,)
    soon = far.at < 4
    for flow in flows:
        if flow.phases and flow.taps:
            if flow is far and put_off:
                @pl.when(soon)
                def _():
                    send_rest(far)
            else:
                send_rest(flow)

    if isinstance(far, Pairs):
        @pl.when(far.at == 4)
        def _():
            @pl.loop(CHUNKS - TURNED, CHUNKS)
            def _(chunk):
                copy(0, far.base + 6, chunk, far.sends + 4, far.device(-1)).start()

    @pl.when(early_edge)
    def _():
        pl.semaphore_wait(ready_sem, 1)

        @pl.loop(0, 0 if isinstance(far, Pairs) else HALF)
        def _(two):
            chunk = 2 * two + (far.at == 0).astype(jnp.int32)
            there, _ = far.first(chunk)
            copy(0, far.base + there, chunk, far.sends, over).start()

    total[...] = jnp.zeros_like(total)
    losses[...] = jnp.zeros_like(losses)

    scale, bias = scale_ref[0], bias_ref[0]
    tasks = agenda(blocks)
    ends = [max(k for k, t in enumerate(tasks) if t[2] == side) for side in range(2)]
    where = [0] + [flow.base + buffer for flow, buffer, _ in blocks]
    waits = [0] + [{"near": 2, "far": 2, "passed": 0}.get(how, 1) for _, _, how in blocks]

    def finish(side):
        @pl.loop(0, CHUNKS // 2)
        def _(chunk):
            part = rows(ROWS - ROWS * side + chunk * SLICE, SLICE)
            direction = scale * total[part, :]
            scaled = 1.0 / norms[part, :]
            unit = raw[part, :].astype(jnp.float32) * scaled
            inner = jnp.sum(unit * direction, axis=-1, keepdims=True)
            total[part, :] = (direction - unit * inner) * scaled

    def pair(task):
        block = pick(task, [t[1] for t in tasks])
        piece = pick(task, [t[2] for t in tasks])
        buffer = pick(block, where)

        @pl.when(pick(block, waits) == 1)
        def _():
            for chunk in range(HALF):
                arrived(buffer, HALF * piece + chunk)

        for number, (flow, _, how) in enumerate(blocks, 1):
            if waits[number] == 2:
                @pl.when(block == number)
                def _(flow=flow, tap=("near", "far").index(how)):
                    for chunk in range(0, HALF, 2):
                        arrived(buffer, HALF * piece + chunk + flow.side(tap))

        side = piece
        mine = rows(ROWS - ROWS * side, ROWS)
        other = held[buffer, rows(piece * PIECE, PIECE), :]
        logits = scale * lax.dot_general(
            held[0, mine, :], other, (((1,), (1,)), ((), ())), preferred_element_type=jnp.float32
        ) + bias
        row = lax.broadcasted_iota(jnp.int32, logits.shape, 0)
        column = lax.broadcasted_iota(jnp.int32, logits.shape, 1)
        diagonal = row == jnp.where(block == 0, column, -1)
        logits = jnp.where(diagonal, -logits, logits)
        small = jnp.exp(-jnp.abs(logits))
        share = 1.0 / (1.0 + small)
        coef = jnp.where(logits >= 0, share, small * share)
        coef = jnp.where(diagonal, -coef, coef)
        loss = jnp.maximum(logits, 0.0) + jnp.log1p(small)
        losses[...] += jnp.where(side == 0, loss, 0.0)
        total[mine, :] += jnp.dot(coef.astype(jnp.bfloat16), other, preferred_element_type=jnp.float32)

        @pl.when((task == ends[0]) | (task == ends[1]))
        def _():
            finish(side)

    due = [sum(t[0] < step for t in tasks) for step in range(STEPS + 2)]

    @pl.loop(0, STEPS + 1)
    def _(step):
        phase = div(step, CHUNKS) + 1
        chunk = rem(step, CHUNKS)
        for flow in flows:
            if flow.phases:
                here_too = phase <= flow.phases
                if flow.turned:
                    @pl.when(here_too & flow.turns(chunk) & (flow.at == 4 - phase))
                    def _(flow=flow):
                        arrived(flow.base + 4, chunk)
                        there = jnp.where(phase == 3, flow.final, 4)
                        copy(flow.base + 4, flow.base + there, chunk, flow.sends + 4, flow.device(-1)).start()

                    here_too &= jnp.logical_not(flow.turns(chunk) & (flow.at == 4 + phase))

                if isinstance(flow, Pairs):
                    turned = flow.turns(chunk)

                    @pl.when(here_too & turned & (flow.at == 4 - phase))
                    def _(flow=flow):
                        arrived(flow.base + 6, chunk)
                        there = jnp.where(phase == 3, flow.final, 6)
                        copy(flow.base + 6, flow.base + there, chunk, flow.sends + 4, flow.device(-1)).start()

                    @pl.when((phase == 3) & turned & (flow.at == 6))
                    def _(flow=flow):
                        arrived(flow.base + 2, chunk)

                    here_too &= jnp.logical_not((phase == 3) & turned & (flow.at >= 6))

                @pl.when(here_too)
                def _(flow=flow):
                    here, there, device = flow.hop(phase, chunk)
                    arrived(flow.base + here, chunk)
                    copy(flow.base + here, flow.base + there, chunk, flow.sends + phase, device).start()

        if put_off:
            @pl.when((step == STEPS - 1) & jnp.logical_not(soon))
            def _():
                send_rest(far)

        @pl.loop(pick(step, due), pick(step + 1, due))
        def _(task):
            pair(task)

    loss_out[...] = jnp.sum(losses[...].T, axis=0, keepdims=True)
    def sent(send, count):
        part = pl.ds(0, count)
        pltpu.make_async_remote_copy(
            src_ref=held.at[0, part], dst_ref=held.at[1, part], send_sem=send_sem.at[send],
            recv_sem=recv_sem.at[1, 0], device_id=(me,), device_id_type=MESH,
        ).wait_send()

    for flow in flows:
        for phase in range(flow.phases + 1):
            if phase and flow.turned:
                @pl.when(flow.at == 4 + phase)
                def _(flow=flow, phase=phase):
                    sent(flow.sends + phase, BOTH - 2 * SLICE)

                @pl.when(flow.at != 4 + phase)
                def _(flow=flow, phase=phase):
                    sent(flow.sends + phase, BOTH)
            elif phase == 3 and isinstance(flow, Pairs):
                @pl.when(flow.at >= 6)
                def _(flow=flow):
                    sent(flow.sends + 3, BOTH - TURNED * SLICE)

                @pl.when(flow.at < 6)
                def _(flow=flow):
                    sent(flow.sends + 3, BOTH)
            else:
                sent(flow.sends + phase, BOTH)
        for number in range(len(getattr(flow, "taps", ()))):
            sent(flow.sends + 4 + number, ROWS)
        if isinstance(flow, Pairs):
            @pl.when((flow.at > 0) & (flow.at < 5))
            def _(flow=flow):
                sent(flow.sends + 4, TURNED * SLICE)

        elif flow.phases and flow.turned:
            @pl.when((flow.at > 0) & (flow.at < 4))
            def _(flow=flow):
                sent(flow.sends + 4, 2 * SLICE)


def hand_over(losses, grads, losses_out, image_out, text_out, sems):
    sources = (losses, grads.at[pl.ds(ROWS, ROWS)], grads.at[pl.ds(0, ROWS)])
    places = (losses_out, image_out, text_out)
    copies = [pltpu.make_async_copy(src, dst, sems.at[k]) for k, (src, dst) in enumerate(zip(sources, places))]
    for copy in copies:
        copy.start()
    for copy in copies:
        copy.wait()


def moved(losses, grads):
    half = jax.ShapeDtypeStruct((ROWS, grads.shape[1]), grads.dtype)
    return pl.pallas_call(
        hand_over,
        out_shape=(jax.ShapeDtypeStruct(losses.shape, losses.dtype), half, half),
        in_specs=[pl.BlockSpec(memory_space=pl.ANY)] * 2,
        out_specs=(pl.BlockSpec(memory_space=pl.ANY),) * 3,
        scratch_shapes=[pltpu.SemaphoreType.DMA((3,))],
        name="moved",
    )(losses, grads)


def window(number, image, text, scale, bias):
    bits = (*WINDOWS[number], TOP_BIT)
    flows, _ = routes(bits)
    buffers = 1 + sum(flow.buffers for flow in flows)
    width = image.shape[1]
    any_space = pl.BlockSpec(memory_space=pl.ANY)
    scalar = pl.BlockSpec(memory_space=pltpu.SMEM)
    return pl.pallas_call(
        functools.partial(kernel, bits),
        out_shape=(
            jax.ShapeDtypeStruct((1, ROWS), jnp.float32),
            jax.ShapeDtypeStruct((BOTH, width), jnp.float32),
        ),
        in_specs=[any_space, any_space, scalar, scalar],
        out_specs=(pl.BlockSpec(memory_space=pltpu.VMEM), pl.BlockSpec(memory_space=pltpu.VMEM)),
        scratch_shapes=[
            pltpu.VMEM((BOTH, width), jnp.bfloat16),
            pltpu.VMEM((BOTH, 1), jnp.float32),
            pltpu.VMEM((buffers, BOTH, width), jnp.bfloat16),
            pltpu.VMEM((ROWS, ROWS), jnp.float32),
            pltpu.SemaphoreType.DMA((2,)),
            pltpu.SemaphoreType.DMA((6 * len(flows),)),
            pltpu.SemaphoreType.DMA((buffers, CHUNKS)),
            pltpu.SemaphoreType.REGULAR,
        ],
        compiler_params=pltpu.CompilerParams(
            collective_id=number, has_side_effects=True, vmem_limit_bytes=24 << 20
        ),
        name="window",
    )(image, text, scale, bias)


def per_device(image, text, plan, offset, logit_scale, logit_bias):
    column = plan[:, :1]
    listed = lax.broadcasted_iota(jnp.int32, column.shape, 0) - offset[0]
    others = jnp.sum(jnp.where((listed >= 0) & (listed < ROUNDS), column, 0)) - (1 << TOP_BIT)
    high = 31 - lax.clz(others)
    low = 31 - lax.clz(others - jnp.left_shift(jnp.int32(1), high))
    number = lax.shift_right_logical(high * (high - 1), jnp.int32(1)) + low
    branches = [functools.partial(window, k) for k in range(len(WINDOWS))]
    losses, image_grad, text_grad = moved(
        *lax.switch(number, branches, image, text, logit_scale, logit_bias)
    )
    return losses.reshape(ROWS), image_grad, text_grad


def solution(mesh):
    in_specs = (P("dp", None), P("dp", None), P(), P(), P(), P())
    out_specs = (P("dp"), P("dp", None), P("dp", None))
    return jax.shard_map(
        per_device, mesh=mesh, in_specs=in_specs, out_specs=out_specs, check_vma=False
    )
```
